32 devices in a mesh: row: 4 (over z), col: 8 (over y, x, core).
Axes of the slice: x: 2, y: 2, z: 4, core: 2. Of those that a mesh axis runs over, the one named last changes fastest.
Arguments:
- start_basis: float32 [4096, 128], P(('row', 'col'))
- tile_values: bfloat16 [4, 8, 16, 128, 128], P('row', 'col')
- tile_coords: int32 [4, 8, 2, 16], P('row', 'col'), may hold values from 0 to 7, as said below
- tile_count: int32 [4, 8], P('row', 'col'), may hold values from 1 to 16, as said below
Outputs:
- basis: float32 [4096, 128], P(('row', 'col'))
- residual: float32 [4096, 128], P(('row', 'col'))
The draws below stay inside these ranges and needn't reach their ends.
Inputs may be any that keep to these rules, and one draw needn't show every extreme that they name: `tile_coords`: on grid position (r, c), slot s < tile_count[r, c] is a tile; local block rows run below 4 and local block columns below 8; slot 0 holds the diagonal tile, local block row r and local block column c; places may repeat, and slots past the count hold arbitrary places. `tile_count`: some device holds 16 tiles and some only its 1 diagonal ones.
All inputs are finite; a program needn't handle non-finite values.
Results may differ from the reference program's by a relative error of at most 0.0021.
The reference program's roundings to bfloat16 on the way (of `scaled`) count: a program that leaves them out, or rounds other values in their place, can miss the bound.
Values may be sent and summed in bfloat16 or wider, within the bound.
No kernel may reach another device: no remote copies, remote signals or barrier semaphores. Data moves between devices by JAX's collectives and lax.ppermute only.
A program may use at most 64 MiB of HBM per device.

```python
import math
import jax
import jax.numpy as jnp
from jax import lax

BR_DEV = 1
TILE = 128
K = 128
EXTRA = 15
ITERS = 3
ROW_GROUPS = 4
COL_GROUPS = 8
ROW_BLOCKS = 4
COL_BLOCKS = 8
N_ITEMS = 4096


def layout(key):
    devices = ROW_GROUPS * COL_GROUPS
    slot_count = BR_DEV + EXTRA
    key_extra, key_pick, key_low, key_rows, key_left, key_right, key_order = jax.random.split(key, 7)
    extra_draw = jax.random.randint(key_extra, (devices,), 0, EXTRA + 1)
    extra_tiles = extra_draw * extra_draw // EXTRA
    busiest = jax.random.randint(key_pick, (), 0, devices)
    quietest = (busiest + 1 + jax.random.randint(key_low, (), 0, devices - 1)) % devices
    device_ids = jnp.arange(devices, dtype=jnp.int32)
    extra_tiles = jnp.where(device_ids == busiest, EXTRA, extra_tiles)
    extra_tiles = jnp.where(device_ids == quietest, 0, extra_tiles)
    tile_totals = (BR_DEV + extra_tiles).astype(jnp.int32).reshape(ROW_GROUPS, COL_GROUPS)
    slot_ids = jnp.arange(slot_count, dtype=jnp.int32)[None, None, :]
    rank_ids = jnp.arange(ROW_GROUPS, dtype=jnp.int32)[:, None, None]
    place_ids = jnp.arange(COL_GROUPS, dtype=jnp.int32)[None, :, None]
    shape_all = (ROW_GROUPS, COL_GROUPS, slot_count)
    random_rows = jax.random.randint(key_rows, shape_all, 0, ROW_BLOCKS)
    left_draw = jax.random.randint(key_left, shape_all, 0, COL_BLOCKS)
    right_draw = jax.random.randint(key_right, shape_all, 0, COL_BLOCKS)
    column_order = jax.random.permutation(key_order, COL_BLOCKS)
    random_cols = column_order[left_draw * right_draw // COL_BLOCKS]
    diagonal = slot_ids < BR_DEV
    local_rows = jnp.where(diagonal, rank_ids * BR_DEV + slot_ids, random_rows).astype(jnp.int32)
    local_cols = jnp.where(diagonal, place_ids * BR_DEV + slot_ids, random_cols).astype(jnp.int32)
    return (local_rows, local_cols, tile_totals)


def draw_tile_coords(key, part):
    local_rows, local_cols, tile_totals = layout(key)
    return jnp.stack([local_rows, local_cols], axis=2)


def draw_tile_count(key, part):
    local_rows, local_cols, tile_totals = layout(key)
    return tile_totals


def draw_tile_values(key, part):
    local_rows, local_cols, tile_totals = layout(key)
    key = jax.random.fold_in(key, 13)
    key_entries, key_rowscale, key_colscale = jax.random.split(key, 3)
    slot_count = BR_DEV + EXTRA
    rank_ids = jnp.arange(ROW_GROUPS, dtype=jnp.int32)[:, None, None]
    place_ids = jnp.arange(COL_GROUPS, dtype=jnp.int32)[None, :, None]
    global_rows = (local_rows // BR_DEV * COL_GROUPS + place_ids) * BR_DEV + local_rows % BR_DEV
    global_cols = rank_ids * COL_BLOCKS + local_cols
    offsets = jnp.arange(TILE, dtype=jnp.int32)
    row_items = global_rows[..., None] * TILE + offsets
    col_items = global_cols[..., None] * TILE + offsets
    item_ids = jnp.arange(N_ITEMS, dtype=jnp.int32)
    col_group = (item_ids // (COL_BLOCKS * TILE)).astype(jnp.float32)
    col_rise = jnp.sqrt(1.0 + 2.0 * col_group / (ROW_GROUPS - 1))
    row_place = (item_ids // (BR_DEV * TILE) % COL_GROUPS).astype(jnp.float32)
    row_rise = jnp.sqrt(1.0 + 2.0 * row_place / (COL_GROUPS - 1))
    shape_all = (ROW_GROUPS, COL_GROUPS, slot_count, TILE, TILE)
    entries = jax.random.truncated_normal(key_entries, -4.0, 4.0, shape_all, jnp.float32)
    row_spread = jnp.exp(jax.random.uniform(key_rowscale, (N_ITEMS,), jnp.float32, 0.0, math.log(10.0)))
    col_spread = jnp.exp(jax.random.uniform(key_colscale, (N_ITEMS,), jnp.float32, 0.0, math.log(10.0)))
    row_factor = (row_spread * row_rise)[row_items]
    col_factor = (col_spread * col_rise)[col_items]
    return (entries * row_factor[..., :, None] * col_factor[..., None, :]).astype(jnp.bfloat16)


def draw_start_basis(key, part):
    key = jax.random.fold_in(key, 14)
    key_entries, key_rough = jax.random.split(key, 2)
    devices = ROW_GROUPS * COL_GROUPS
    panel_ids = (jnp.arange(N_ITEMS, dtype=jnp.int32) // (BR_DEV * TILE)).astype(jnp.float32)
    rising = 1.0 + 2.0 * panel_ids / (devices - 1)
    roughness = jnp.exp(jax.random.uniform(key_rough, (N_ITEMS, 1), jnp.float32, 0.0, math.log(3.0)))
    entries = jax.random.normal(key_entries, (N_ITEMS, K), jnp.float32)
    return entries * roughness * rising[:, None]


def setup_inputs(seed: int = 0) -> dict:
    seeds = jax.random.split(jax.random.key(seed), 5)
    return {
        "start_basis": draw_start_basis(jax.random.fold_in(seeds[4], 71), 0),
        "tile_values": draw_tile_values(jax.random.fold_in(seeds[4], 71), 0),
        "tile_coords": draw_tile_coords(jax.random.fold_in(seeds[4], 71), 0),
        "tile_count": draw_tile_count(jax.random.fold_in(seeds[4], 71), 0),
    }


EPSILON = 1e-06
STEP_SIZE = 0.5
MOMENTUM = 0.5

def moments(left_side, right_side):
    return jnp.dot(left_side.T.astype(jnp.float32), right_side.astype(jnp.float32), preferred_element_type=jnp.float32, precision=lax.Precision.HIGHEST) / N_ITEMS

def orthonormal(moved):
    factor = jnp.linalg.cholesky(moments(moved, moved))
    inverse = lax.linalg.triangular_solve(factor, jnp.eye(K, dtype=jnp.float32), left_side=True, lower=True)
    return jnp.dot(moved, inverse.T, precision=lax.Precision.HIGHEST)

def placements(tile_coords, tile_count):
    devices = ROW_GROUPS * COL_GROUPS
    slot_count = BR_DEV + EXTRA
    device_ids = jnp.arange(devices, dtype=jnp.int32)
    rank_ids = (device_ids // COL_GROUPS)[:, None]
    place_ids = (device_ids % COL_GROUPS)[:, None]
    local_rows = tile_coords[:, :, 0, :].reshape(devices, slot_count)
    local_cols = tile_coords[:, :, 1, :].reshape(devices, slot_count)
    global_rows = (local_rows // BR_DEV * COL_GROUPS + place_ids) * BR_DEV + local_rows % BR_DEV
    global_cols = rank_ids * COL_BLOCKS + local_cols
    slot_ids = jnp.arange(slot_count, dtype=jnp.int32)[None, :]
    live_slots = (slot_ids < tile_count.reshape(devices, 1)).astype(jnp.float32)
    return (global_rows.astype(jnp.int32), global_cols.astype(jnp.int32), live_slots)

def energies(tile_blocks, global_rows, global_cols, live_slots):
    blocks_total = N_ITEMS // TILE

    def visit_device(running, inputs):
        row_energy, col_energy = running
        tiles_here, rows_here, cols_here, live_here = inputs
        widened = tiles_here.astype(jnp.float32)
        squared = widened * widened
        row_terms = jnp.sum(squared, axis=2) * live_here[:, None]
        col_terms = jnp.sum(squared, axis=1) * live_here[:, None]
        return ((row_energy.at[rows_here].add(row_terms), col_energy.at[cols_here].add(col_terms)), None)
    initial = (jnp.zeros((blocks_total, TILE), jnp.float32), jnp.zeros((blocks_total, TILE), jnp.float32))
    finals, unused = lax.scan(visit_device, initial, (tile_blocks, global_rows, global_cols, live_slots))
    return (finals[0].reshape(N_ITEMS), finals[1].reshape(N_ITEMS))

def product(tile_blocks, global_rows, global_cols, live_slots, scaled):
    blocks_total = N_ITEMS // TILE
    panels = scaled.reshape(blocks_total, TILE, K)

    def visit_device(running, inputs):
        tiles_here, rows_here, cols_here, live_here = inputs
        picked = panels[cols_here].astype(jnp.float32)
        products = jnp.einsum('sab,sbk->sak', tiles_here.astype(jnp.float32), picked, precision=lax.Precision.HIGHEST)
        return (running.at[rows_here].add(products * live_here[:, None, None]), None)
    initial = jnp.zeros((blocks_total, TILE, K), jnp.float32)
    applied, unused = lax.scan(visit_device, initial, (tile_blocks, global_rows, global_cols, live_slots))
    return applied.reshape(N_ITEMS, K)

def reference(start_basis, tile_values, tile_coords, tile_count):
    devices = ROW_GROUPS * COL_GROUPS
    tile_blocks = tile_values.reshape(devices, BR_DEV + EXTRA, TILE, TILE)
    global_rows, global_cols, live_slots = placements(tile_coords, tile_count)
    row_energy, col_energy = energies(tile_blocks, global_rows, global_cols, live_slots)
    row_scale = (row_energy + EPSILON) ** (-0.25)
    col_scale = (col_energy + EPSILON) ** (-0.25)
    current = orthonormal(start_basis)
    previous = jnp.zeros_like(start_basis)
    residual = previous
    for iteration in range(ITERS):
        scaled = (col_scale[:, None] * current).astype(jnp.bfloat16)
        applied = row_scale[:, None] * product(tile_blocks, global_rows, global_cols, live_slots, scaled)
        rayleigh = moments(current, applied)
        coupling = moments(current, previous)
        residual = applied - jnp.dot(current, rayleigh, precision=lax.Precision.HIGHEST)
        direction = residual + MOMENTUM * (previous - jnp.dot(current, coupling, precision=lax.Precision.HIGHEST))
        current = orthonormal(current + STEP_SIZE * direction)
        previous = direction
    return (current, residual)
```

```python
import functools

import jax
import jax.numpy as jnp
from jax import lax
from jax.experimental import pallas as pl
from jax.experimental.pallas import tpu as pltpu
from jax.sharding import PartitionSpec as P

ITERS = 3
EPSILON = 1e-06
STEP_SIZE = 0.5
MOMENTUM = 0.5

SUB = 8
F32 = jnp.float32
BF16 = jnp.bfloat16
HIGHEST = lax.Precision.HIGHEST
VMEM = pl.BlockSpec(memory_space=pltpu.VMEM)
SMEM = pl.BlockSpec(memory_space=pltpu.SMEM)
PARAMS = pltpu.CompilerParams(vmem_limit_bytes=40 * 2**20)


def call(body, outputs, scratch=(), smem=1, inputs=0):
    return pl.pallas_call(
        body,
        out_shape=[jax.ShapeDtypeStruct(shape, dtype) for shape, dtype in outputs],
        in_specs=[SMEM] * smem + [VMEM] * (inputs - smem),
        out_specs=[VMEM] * len(outputs),
        scratch_shapes=list(scratch),
        compiler_params=PARAMS,
    )


def dot(left, right, contract=((1,), (0,)), precision=HIGHEST):
    return lax.dot_general(
        left, right, (contract, ((), ())), precision=precision, preferred_element_type=F32
    )


def swap(value, axis, distance):
    size = lax.axis_size(axis)
    return lax.ppermute(value, axis, [(i, i ^ distance) for i in range(size)])


def gather_pieces(value):
    size = lax.axis_size("col")
    even = [value] + [swap(value, "col", k) for k in range(2, size, 2)]
    odd = [swap(piece, "col", 1) for piece in even]
    return [piece for pair in zip(even, odd) for piece in pair]


def plane_sum(keep, send):
    half = keep + swap(send, "col", 1)
    total = half
    for k in range(2, lax.axis_size("col"), 2):
        total = total + swap(half, "col", k)
    return total, swap(total, "col", 1)


def sub(x, k):
    return jnp.broadcast_to(x[k : k + 1, :], x.shape)


def lane(x, j):
    return jnp.broadcast_to(x[:, j : j + 1], x.shape)


def factor(matrix):
    edge = matrix.shape[0]
    blocks = edge // SUB
    shape = (SUB, edge)
    rows = [matrix[SUB * b : SUB * b + SUB, :] for b in range(blocks)]
    sublane = lax.broadcasted_iota(jnp.int32, shape, 0)
    column = lax.broadcasted_iota(jnp.int32, shape, 1)
    inverse = [jnp.where(column == sublane + SUB * b, 1.0, 0.0).astype(F32) for b in range(blocks)]
    upper_out, inverse_out = [], []
    for b in range(blocks):
        cols = [lane(rows[b], SUB * b + k) for k in range(SUB)]
        factors, pivots, pivot_inv, upper = [], [], [], {}
        for k in range(SUB):
            pivot = sub(cols[k], k)
            pivots.append(pivot)
            pivot_inv.append(1.0 / pivot)
            factors.append(jnp.where(sublane > k, cols[k] * pivot_inv[k], 0.0))
            for j in range(k + 1, SUB):
                upper[k, j] = sub(cols[j], k)
                cols[j] = cols[j] - factors[k] * upper[k, j]
        here, inv_here = rows[b], inverse[b]
        row_bcast, inv_bcast = [], []
        for k in range(SUB):
            row_bcast.append(sub(here, k))
            inv_bcast.append(sub(inv_here, k))
            if k < SUB - 1:
                here = here - factors[k] * row_bcast[k]
                inv_here = inv_here - factors[k] * inv_bcast[k]
        pivot = pivots[SUB - 1]
        for k in range(SUB - 1):
            pivot = jnp.where(sublane == k, pivots[k], pivot)
        root_inv = 1.0 / jnp.sqrt(pivot)
        upper_out.append(jnp.where(column >= sublane + SUB * b, here * root_inv, 0.0))
        inverse_out.append(inv_here * root_inv)
        for p in range(b + 1, blocks):
            terms = [lane(rows[p], SUB * b + k) for k in range(SUB)]
            row_p, inv_p = rows[p], inverse[p]
            for k in range(SUB):
                scale = terms[k] * pivot_inv[k]
                for j in range(k + 1, SUB):
                    terms[j] = terms[j] - scale * upper[k, j]
                row_p = row_p - scale * row_bcast[k]
                inv_p = inv_p - scale * inv_bcast[k]
            rows[p], inverse[p] = row_p, inv_p
    return jnp.concatenate(upper_out, axis=0), jnp.concatenate(inverse_out, axis=0)


def energy_kernel(sizes, places, tiles, start, codes, message, row_sums, col_sums):
    edge, slots, n_row, n_col, row_pad = sizes
    row_sums[...] = jnp.zeros_like(row_sums)
    col_sums[...] = jnp.zeros_like(col_sums)
    ones = jnp.ones((SUB, edge), BF16)

    def visit(s, carry):
        wide = tiles[s].astype(F32)
        square = wide * wide
        high = square.astype(BF16)
        low = (square - high.astype(F32)).astype(BF16)
        by_row = ((1,), (1,))
        by_col = ((1,), (0,))
        fast = lax.Precision.DEFAULT
        u = jnp.minimum(places[s], n_row - 1)
        v = jnp.minimum(places[slots + s], n_col - 1)
        row_sums[u] += dot(ones, high, by_row, fast) + dot(ones, low, by_row, fast)
        col_sums[v] += dot(ones, high, by_col, fast) + dot(ones, low, by_col, fast)
        return carry

    lax.fori_loop(0, places[2 * slots], visit, 0)
    message[0:edge, :] = start[...]
    for v in range(n_col):
        message[edge + v : edge + v + 1, :] = col_sums[v, 0:1, :]
    base = edge + n_col
    for u in range(n_row):
        message[base + u : base + u + 1, :] = row_sums[u, 0:1, :]
    for u in range(n_row, row_pad):
        message[base + u : base + u + 1, :] = row_sums[0, 0:1, :]
    message[base + row_pad :, :] = codes[...]


def start_kernel(sizes, here, *refs):
    edge, n_row, n_col, row_pad = sizes
    pieces, (basis, keep, send, row_scale, half) = refs[:n_row], refs[n_row:]
    rank, core = here[0], here[1] % 2
    gram = jnp.zeros((edge, edge), F32)
    row_energy = jnp.zeros((row_pad, edge), F32)
    part = n_row * n_col // 2
    for k in range(n_row):
        group = rank ^ k
        rows = pieces[k][0:edge, :]
        basis[pl.ds(pl.multiple_of(group * edge, edge), edge), :] = rows
        gram += dot(rows, rows, ((0,), (0,)))
        row_energy += pieces[k][edge + n_col : edge + n_col + row_pad, :]
        half[pl.ds(pl.multiple_of(edge + group * n_col, n_col), n_col), :] = pieces[k][
            edge : edge + n_col, :
        ]
    half[0:edge, :] = gram
    low = jnp.concatenate([half[0 : edge // 2, :], half[edge : edge + part, :]], axis=0)
    high = jnp.concatenate([half[edge // 2 : edge, :], half[edge + part :, :]], axis=0)
    keep[...] = jnp.where(core == 0, low, high)
    send[...] = jnp.where(core == 0, high, low)
    scale = inverse_fourth_root(row_energy)
    for u in range(n_row):
        row_scale[u * edge : (u + 1) * edge, :] = down_rows(scale[u : u + 1, :], edge)


def inverse_fourth_root(energy):
    return 1.0 / jnp.sqrt(jnp.sqrt(energy + EPSILON))


def down_rows(row, edge):
    return jnp.transpose(jnp.broadcast_to(row, (edge, edge)))


def halves(here, mine, other):
    core = here[1] % 2
    own, sibling = mine[...], other[...]
    return jnp.where(core == 0, own, sibling), jnp.where(core == 0, sibling, own)


def first_kernel(sizes, here, mine, other, basis, current, scaled, col_scale, energy):
    edge, n_row, n_col, items = sizes
    low, high = halves(here, mine, other)
    gram = jnp.concatenate([low[: edge // 2], high[: edge // 2]], axis=0) / items
    energy[...] = jnp.concatenate([low[edge // 2 :], high[edge // 2 :]], axis=0)
    for u in range(n_row):
        row = energy[pl.ds(u * n_col + here[1], 1), :]
        col_scale[u * edge : (u + 1) * edge, :] = down_rows(inverse_fourth_root(row), edge)
    _, inverse = factor(gram)
    value = dot(basis[...], inverse, ((1,), (1,)))
    current[...] = value
    scaled[...] = (col_scale[...] * value).astype(BF16)


def apply_kernel(sizes, first, meta, here, tiles, row_scale, current, previous, *refs):
    edge, slots, n_row, n_col, unroll = sizes
    pieces, (value, keep, send, panels, total) = refs[:n_col], refs[n_col:]
    rank, place = here[0], here[1]
    for k in range(n_col):
        panels[place ^ k] = pieces[k][...].reshape(n_row, edge, edge)
    total[...] = jnp.zeros_like(total)
    width = slots + 1
    for k in range(n_row):
        group = rank ^ k
        count = meta[k * width + slots]

        def visit(q, carry, k=k, group=group, count=count):
            for j in range(unroll):
                s = q * unroll + j
                code = meta[k * width + s]
                u = jnp.minimum(code // n_col, n_row - 1)
                v = code % n_col
                product = dot(
                    tiles[group * slots + s],
                    panels[v, group],
                    precision=lax.Precision.DEFAULT,
                )
                total[u] += jnp.where(s < count, product, 0.0)
            return carry

        lax.fori_loop(0, (count + unroll - 1) // unroll, visit, 0)
    applied = row_scale[...] * total[...].reshape(n_row * edge, edge)
    moved = applied if first else applied + MOMENTUM * previous[...]
    value[...] = moved
    cross = dot(current[...], moved, ((0,), (0,)))
    square = dot(moved, moved, ((0,), (0,)))
    core = place % 2
    keep[...] = jnp.where(core == 0, cross, square)
    send[...] = jnp.where(core == 0, square, cross)


def moved_gram(cross, square):
    edge = cross.shape[0]
    shape = (edge, edge)
    row = lax.broadcasted_iota(jnp.int32, shape, 0)
    column = lax.broadcasted_iota(jnp.int32, shape, 1)
    identity = jnp.where(row == column, 1.0, 0.0).astype(F32)
    change = square - dot(cross, cross, ((0,), (0,)))
    return identity + STEP_SIZE * STEP_SIZE * change


def update_kernel(
    items, here, mine, other, current, value, col_scale, new, scaled, direction, coupling
):
    cross, square = halves(here, mine, other)
    cross, square = cross / items, square / items
    step = value[...] - dot(current[...], cross)
    direction[...] = step
    upper, inverse = factor(moved_gram(cross, square))
    coupling[...] = (upper - inverse) / STEP_SIZE
    result = dot(current[...] + STEP_SIZE * step, inverse, ((1,), (1,)))
    new[...] = result
    scaled[...] = (col_scale[...] * result).astype(BF16)


def last_kernel(
    sizes, here, mine, other, current, value, previous, coupling, basis, residual
):
    edge, items = sizes
    cross, square = halves(here, mine, other)
    cross, square = cross / items, square / items
    rows = pl.ds(pl.multiple_of(here[0] * edge, edge), edge)
    old, moved = current[rows, :], value[rows, :]
    rayleigh = cross - MOMENTUM * coupling[...]
    residual[...] = moved - MOMENTUM * previous[rows, :] - dot(old, rayleigh)
    step = moved - dot(old, cross)
    _, inverse = factor(moved_gram(cross, square))
    basis[...] = dot(old + STEP_SIZE * step, inverse, ((1,), (1,)))


def per_device(start_basis, tile_values, tile_coords, tile_count):
    edge, columns = start_basis.shape
    tiles = tile_values[0, 0]
    slots = tiles.shape[0]
    n_row, n_col = lax.axis_size("row"), lax.axis_size("col")
    items = float(edge * n_row * n_col)
    rows = n_row * edge
    row_pad = -(-n_row // SUB) * SUB
    here = jnp.stack([lax.axis_index("row"), lax.axis_index("col")]).astype(jnp.int32)
    block = ((rows, columns), F32)
    square = ((columns, columns), F32)

    all_tiles = lax.all_gather(tiles, "row", axis=0, tiled=True)

    places = jnp.concatenate([tile_coords[0, 0].reshape(-1), tile_count[0]])
    codes = jnp.concatenate([tile_coords[0, 0, 0] * n_col + tile_coords[0, 0, 1], tile_count[0]])
    codes = jnp.pad(codes.astype(F32)[None, :], ((0, SUB - 1), (0, columns - slots - 1)))
    length = edge + n_col + row_pad + SUB
    (message,) = call(
        functools.partial(energy_kernel, (edge, slots, n_row, n_col, row_pad)),
        [((length, columns), F32)],
        [pltpu.VMEM((n_row, SUB, columns), F32), pltpu.VMEM((n_col, SUB, columns), F32)],
        inputs=4,
    )(places, tiles, start_basis, codes)
    messages = [message] + [swap(message, "row", k) for k in range(1, n_row)]
    meta = jnp.concatenate([m[length - SUB, : slots + 1] for m in messages]).astype(jnp.int32)

    part = (edge + n_row * n_col) // 2
    basis, keep, send, row_scale = call(
        functools.partial(start_kernel, (edge, n_row, n_col, row_pad)),
        [block, ((part, columns), F32), ((part, columns), F32), block],
        [pltpu.VMEM((2 * part, columns), F32)],
        inputs=1 + n_row,
    )(here, *messages)
    mine, other = plane_sum(keep, send)
    current, scaled, col_scale = call(
        functools.partial(first_kernel, (edge, n_row, n_col, items)),
        [block, ((rows, columns), BF16), block],
        [pltpu.VMEM((n_row * n_col, columns), F32)],
        inputs=4,
    )(here, mine, other, basis)

    previous, coupling = current, None
    for iteration in range(ITERS):
        pieces = gather_pieces(scaled)
        value, keep, send = call(
            functools.partial(apply_kernel, (edge, slots, n_row, n_col, 4), iteration == 0),
            [block, square, square],
            [
                pltpu.VMEM((n_col, n_row, edge, columns), BF16),
                pltpu.VMEM((n_row, edge, columns), F32),
            ],
            smem=2,
            inputs=6 + n_col,
        )(meta, here, all_tiles, row_scale, current, previous, *pieces)
        mine, other = plane_sum(keep, send)
        if iteration == ITERS - 1:
            break
        current, scaled, previous, coupling = call(
            functools.partial(update_kernel, items),
            [block, ((rows, columns), BF16), block, square],
            inputs=6,
        )(here, mine, other, current, value, col_scale)
    basis, residual = call(
        functools.partial(last_kernel, (edge, items)),
        [((edge, columns), F32), ((edge, columns), F32)],
        inputs=7,
    )(here, mine, other, current, value, previous, coupling)
    return (basis, residual)


def solution(mesh):
    return jax.shard_map(
        per_device,
        mesh=mesh,
        in_specs=(
            P(("row", "col"), None),
            P("row", "col", None, None, None),
            P("row", "col", None, None),
            P("row", "col"),
        ),
        out_specs=(P(("row", "col"), None), P(("row", "col"), None)),
        check_vma=False,
    )
```

```python
import functools

import jax
import jax.numpy as jnp
from jax import lax
from jax.experimental import pallas as pl
from jax.experimental.pallas import tpu as pltpu
from jax.sharding import PartitionSpec as P

ITERS = 3
EPSILON = 1e-06
STEP_SIZE = 0.5
MOMENTUM = 0.5

SUB = 8
F32 = jnp.float32
BF16 = jnp.bfloat16
HIGHEST = lax.Precision.HIGHEST
VMEM = pl.BlockSpec(memory_space=pltpu.VMEM)
SMEM = pl.BlockSpec(memory_space=pltpu.SMEM)
PARAMS = pltpu.CompilerParams(vmem_limit_bytes=40 * 2**20)


def call(body, outputs, scratch=(), smem=1, inputs=0):
    return pl.pallas_call(
        body,
        out_shape=[jax.ShapeDtypeStruct(shape, dtype) for shape, dtype in outputs],
        in_specs=[SMEM] * smem + [VMEM] * (inputs - smem),
        out_specs=[VMEM] * len(outputs),
        scratch_shapes=list(scratch),
        compiler_params=PARAMS,
    )


def dot(left, right, contract=((1,), (0,)), precision=HIGHEST):
    return lax.dot_general(
        left, right, (contract, ((), ())), precision=precision, preferred_element_type=F32
    )


def swap(value, axis, distance):
    size = lax.axis_size(axis)
    return lax.ppermute(value, axis, [(i, i ^ distance) for i in range(size)])


def gather_pieces(value):
    size = lax.axis_size("col")
    even = [value] + [swap(value, "col", k) for k in range(2, size, 2)]
    odd = [swap(piece, "col", 1) for piece in even]
    return [piece for pair in zip(even, odd) for piece in pair]


def plane_sum(keep, send):
    half = keep + swap(send, "col", 1)
    total = half
    for k in range(2, lax.axis_size("col"), 2):
        total = total + swap(half, "col", k)
    return total, swap(total, "col", 1)


def sub(x, k):
    return jnp.broadcast_to(x[k : k + 1, :], x.shape)


def lane(x, j):
    return jnp.broadcast_to(x[:, j : j + 1], x.shape)


def factor(matrix):
    edge = matrix.shape[0]
    blocks = edge // SUB
    shape = (SUB, edge)
    rows = [matrix[SUB * b : SUB * b + SUB, :] for b in range(blocks)]
    sublane = lax.broadcasted_iota(jnp.int32, shape, 0)
    column = lax.broadcasted_iota(jnp.int32, shape, 1)
    inverse = [jnp.where(column == sublane + SUB * b, 1.0, 0.0).astype(F32) for b in range(blocks)]
    upper_out, inverse_out = [], []
    for b in range(blocks):
        cols = [lane(rows[b], SUB * b + k) for k in range(SUB)]
        factors, pivots, pivot_inv, upper = [], [], [], {}
        for k in range(SUB):
            pivot = sub(cols[k], k)
            pivots.append(pivot)
            pivot_inv.append(1.0 / pivot)
            factors.append(jnp.where(sublane > k, cols[k] * pivot_inv[k], 0.0))
            for j in range(k + 1, SUB):
                upper[k, j] = sub(cols[j], k)
                cols[j] = cols[j] - factors[k] * upper[k, j]
        here, inv_here = rows[b], inverse[b]
        row_bcast, inv_bcast = [], []
        for k in range(SUB):
            row_bcast.append(sub(here, k))
            inv_bcast.append(sub(inv_here, k))
            if k < SUB - 1:
                here = here - factors[k] * row_bcast[k]
                inv_here = inv_here - factors[k] * inv_bcast[k]
        pivot = pivots[SUB - 1]
        for k in range(SUB - 1):
            pivot = jnp.where(sublane == k, pivots[k], pivot)
        root_inv = 1.0 / jnp.sqrt(pivot)
        upper_out.append(jnp.where(column >= sublane + SUB * b, here * root_inv, 0.0))
        inverse_out.append(inv_here * root_inv)
        for p in range(b + 1, blocks):
            terms = [lane(rows[p], SUB * b + k) for k in range(SUB)]
            row_p, inv_p = rows[p], inverse[p]
            for k in range(SUB):
                scale = terms[k] * pivot_inv[k]
                for j in range(k + 1, SUB):
                    terms[j] = terms[j] - scale * upper[k, j]
                row_p = row_p - scale * row_bcast[k]
                inv_p = inv_p - scale * inv_bcast[k]
            rows[p], inverse[p] = row_p, inv_p
    return jnp.concatenate(upper_out, axis=0), jnp.concatenate(inverse_out, axis=0)


def energy_kernel(sizes, places, counts, tiles, start, message, row_sums, col_sums):
    edge, slots, n_row, n_col, row_pad, unroll = sizes
    count = counts[0, 0]
    row_sums[...] = jnp.zeros_like(row_sums)
    col_sums[...] = jnp.zeros_like(col_sums)
    ones = jnp.ones((SUB, edge), BF16)

    def visit(q, carry):
        for j in range(unroll):
            s = q * unroll + j
            wide = tiles[0, 0, s].astype(F32)
            square = jnp.where(s < count, wide * wide, 0.0)
            high = square.astype(BF16)
            low = (square - high.astype(F32)).astype(BF16)
            by_row = ((1,), (1,))
            by_col = ((1,), (0,))
            fast = lax.Precision.DEFAULT
            u = jnp.minimum(places[0, 0, 0, s], n_row - 1)
            v = jnp.minimum(places[0, 0, 1, s], n_col - 1)
            row_sums[u] += dot(ones, high, by_row, fast) + dot(ones, low, by_row, fast)
            col_sums[v] += dot(ones, high, by_col, fast) + dot(ones, low, by_col, fast)
        return carry

    lax.fori_loop(0, (count + unroll - 1) // unroll, visit, 0)
    message[0:edge, :] = start[...]
    for v in range(n_col):
        message[edge + v : edge + v + 1, :] = col_sums[v, 0:1, :]
    base = edge + n_col
    for u in range(n_row):
        message[base + u : base + u + 1, :] = row_sums[u, 0:1, :]
    for u in range(n_row, row_pad):
        message[base + u : base + u + 1, :] = row_sums[0, 0:1, :]
    column = lax.broadcasted_iota(jnp.int32, (SUB, edge), 1)
    codes = jnp.where(column == slots, count, 0)
    for s in range(slots):
        code = places[0, 0, 0, s] * n_col + places[0, 0, 1, s]
        codes = jnp.where(column == s, code, codes)
    message[base + row_pad :, :] = codes.astype(F32)


def start_kernel(sizes, here, *refs):
    edge, n_row, n_col, row_pad = sizes
    pieces, (basis, keep, send, row_scale, half) = refs[:n_row], refs[n_row:]
    rank, core = here[0], here[1] % 2
    gram = jnp.zeros((edge, edge), F32)
    row_energy = jnp.zeros((row_pad, edge), F32)
    part = n_row * n_col // 2
    for k in range(n_row):
        group = rank ^ k
        rows = pieces[k][0:edge, :]
        basis[pl.ds(pl.multiple_of(group * edge, edge), edge), :] = rows
        gram += dot(rows, rows, ((0,), (0,)))
        row_energy += pieces[k][edge + n_col : edge + n_col + row_pad, :]
        half[pl.ds(pl.multiple_of(edge + group * n_col, n_col), n_col), :] = pieces[k][
            edge : edge + n_col, :
        ]
    half[0:edge, :] = gram
    low = jnp.concatenate([half[0 : edge // 2, :], half[edge : edge + part, :]], axis=0)
    high = jnp.concatenate([half[edge // 2 : edge, :], half[edge + part :, :]], axis=0)
    keep[...] = jnp.where(core == 0, low, high)
    send[...] = jnp.where(core == 0, high, low)
    scale = inverse_fourth_root(row_energy)
    for u in range(n_row):
        row_scale[u * edge : (u + 1) * edge, :] = down_rows(scale[u : u + 1, :], edge)


def inverse_fourth_root(energy):
    return 1.0 / jnp.sqrt(jnp.sqrt(energy + EPSILON))


def down_rows(row, edge):
    return jnp.transpose(jnp.broadcast_to(row, (edge, edge)))


def halves(here, mine, other):
    core = here[1] % 2
    own, sibling = mine[...], other[...]
    return jnp.where(core == 0, own, sibling), jnp.where(core == 0, sibling, own)


def first_kernel(sizes, here, mine, other, basis, current, scaled, col_scale, energy):
    edge, n_row, n_col, items = sizes
    low, high = halves(here, mine, other)
    gram = jnp.concatenate([low[: edge // 2], high[: edge // 2]], axis=0) / items
    energy[...] = jnp.concatenate([low[edge // 2 :], high[edge // 2 :]], axis=0)
    for u in range(n_row):
        row = energy[pl.ds(u * n_col + here[1], 1), :]
        col_scale[u * edge : (u + 1) * edge, :] = down_rows(inverse_fourth_root(row), edge)
    _, inverse = factor(gram)
    value = dot(basis[...], inverse, ((1,), (1,)))
    current[...] = value
    scaled[...] = (col_scale[...] * value).astype(BF16)


def apply_kernel(sizes, first, meta, here, row_scale, current, previous, *refs):
    edge, slots, n_row, n_col, unroll = sizes
    tiles, pieces = refs[: 2 * n_row], refs[2 * n_row : 2 * n_row + n_col]
    value, keep, send, panels, total = refs[2 * n_row + n_col :]
    rank, place = here[0], here[1]
    for k in range(n_col):
        panels[place ^ k] = pieces[k][...].reshape(n_row, edge, edge)
    total[...] = jnp.zeros_like(total)
    width = slots + 1
    for k in range(n_row):
        group = rank ^ k
        for part in range(2):
            begin = part * tiles[0].shape[2]
            live = jnp.clip(meta[k * width + slots] - begin, 0, tiles[part].shape[2])

            def visit(q, carry, k=k, group=group, part=part, begin=begin, live=live):
                for j in range(unroll):
                    s = q * unroll + j
                    code = meta[k * width + begin + s]
                    u = jnp.minimum(code // n_col, n_row - 1)
                    v = code % n_col
                    product = dot(
                        tiles[2 * k + part][0, 0, s],
                        panels[v, group],
                        precision=lax.Precision.DEFAULT,
                    )
                    total[u] += jnp.where(s < live, product, 0.0)
                return carry

            lax.fori_loop(0, (live + unroll - 1) // unroll, visit, 0)
    applied = row_scale[...] * total[...].reshape(n_row * edge, edge)
    moved = applied if first else applied + MOMENTUM * previous[...]
    value[...] = moved
    cross = dot(current[...], moved, ((0,), (0,)))
    square = dot(moved, moved, ((0,), (0,)))
    core = place % 2
    keep[...] = jnp.where(core == 0, cross, square)
    send[...] = jnp.where(core == 0, square, cross)


def moved_gram(cross, square):
    edge = cross.shape[0]
    shape = (edge, edge)
    row = lax.broadcasted_iota(jnp.int32, shape, 0)
    column = lax.broadcasted_iota(jnp.int32, shape, 1)
    identity = jnp.where(row == column, 1.0, 0.0).astype(F32)
    change = square - dot(cross, cross, ((0,), (0,)))
    return identity + STEP_SIZE * STEP_SIZE * change


def update_kernel(
    items, here, mine, other, current, value, col_scale, new, scaled, direction, coupling
):
    cross, square = halves(here, mine, other)
    cross, square = cross / items, square / items
    step = value[...] - dot(current[...], cross)
    direction[...] = step
    upper, inverse = factor(moved_gram(cross, square))
    coupling[...] = (upper - inverse) / STEP_SIZE
    result = dot(current[...] + STEP_SIZE * step, inverse, ((1,), (1,)))
    new[...] = result
    scaled[...] = (col_scale[...] * result).astype(BF16)


def last_kernel(
    sizes, here, mine, other, current, value, previous, coupling, basis, residual
):
    edge, items = sizes
    cross, square = halves(here, mine, other)
    cross, square = cross / items, square / items
    rows = pl.ds(pl.multiple_of(here[0] * edge, edge), edge)
    old, moved = current[rows, :], value[rows, :]
    rayleigh = cross - MOMENTUM * coupling[...]
    residual[...] = moved - MOMENTUM * previous[rows, :] - dot(old, rayleigh)
    step = moved - dot(old, cross)
    _, inverse = factor(moved_gram(cross, square))
    basis[...] = dot(old + STEP_SIZE * step, inverse, ((1,), (1,)))


def per_device(start_basis, tile_values, tile_coords, tile_count):
    edge, columns = start_basis.shape
    slots = tile_values.shape[2]
    n_row, n_col = lax.axis_size("row"), lax.axis_size("col")
    items = float(edge * n_row * n_col)
    rows = n_row * edge
    row_pad = -(-n_row // SUB) * SUB
    here = jnp.stack([lax.axis_index("row"), lax.axis_index("col")]).astype(jnp.int32)
    block = ((rows, columns), F32)
    square = ((columns, columns), F32)

    first = slots * 4 // 16
    halves_here = (tile_values[:, :, :first], tile_values[:, :, first:])
    early, late = ([half] + [None] * (n_row - 1) for half in halves_here)
    direct = [k for k in range(1, n_row) if k & (k - 1) == 0]
    relayed = [k for k in range(1, n_row) if k & (k - 1) != 0]
    for k in direct:
        early[k] = swap(early[0], "row", k)

    length = edge + n_col + row_pad + SUB
    (message,) = call(
        functools.partial(energy_kernel, (edge, slots, n_row, n_col, row_pad, 4)),
        [((length, columns), F32)],
        [pltpu.VMEM((n_row, SUB, columns), F32), pltpu.VMEM((n_col, SUB, columns), F32)],
        smem=2,
        inputs=4,
    )(tile_coords, tile_count, tile_values, start_basis)
    messages = [message] + [swap(message, "row", k) for k in range(1, n_row)]
    messages, early, late[0] = lax.optimization_barrier((messages, early, late[0]))
    for k in relayed:
        early[k] = swap(early[k & (k - 1)], "row", k & -k)
    for k in direct:
        late[k] = swap(late[0], "row", k)
    meta = jnp.concatenate([m[length - SUB, : slots + 1] for m in messages]).astype(jnp.int32)

    part = (edge + n_row * n_col) // 2
    basis, keep, send, row_scale = call(
        functools.partial(start_kernel, (edge, n_row, n_col, row_pad)),
        [block, ((part, columns), F32), ((part, columns), F32), block],
        [pltpu.VMEM((2 * part, columns), F32)],
        inputs=1 + n_row,
    )(here, *messages)
    mine, other = plane_sum(keep, send)
    current, scaled, col_scale = call(
        functools.partial(first_kernel, (edge, n_row, n_col, items)),
        [block, ((rows, columns), BF16), block],
        [pltpu.VMEM((n_row * n_col, columns), F32)],
        inputs=4,
    )(here, mine, other, basis)

    scaled, early, late = lax.optimization_barrier((scaled, early, late))
    for k in relayed:
        late[k] = swap(late[k & (k - 1)], "row", k & -k)
    tiles = [half for pair in zip(early, late) for half in pair]

    previous, coupling = current, None
    for iteration in range(ITERS):
        pieces = gather_pieces(scaled)
        value, keep, send = call(
            functools.partial(apply_kernel, (edge, slots, n_row, n_col, 4), iteration == 0),
            [block, square, square],
            [
                pltpu.VMEM((n_col, n_row, edge, columns), BF16),
                pltpu.VMEM((n_row, edge, columns), F32),
            ],
            smem=2,
            inputs=5 + 2 * n_row + n_col,
        )(meta, here, row_scale, current, previous, *tiles, *pieces)
        mine, other = plane_sum(keep, send)
        if iteration == ITERS - 1:
            break
        current, scaled, previous, coupling = call(
            functools.partial(update_kernel, items),
            [block, ((rows, columns), BF16), block, square],
            inputs=6,
        )(here, mine, other, current, value, col_scale)
    basis, residual = call(
        functools.partial(last_kernel, (edge, items)),
        [((edge, columns), F32), ((edge, columns), F32)],
        inputs=7,
    )(here, mine, other, current, value, previous, coupling)
    return (basis, residual)


def solution(mesh):
    return jax.shard_map(
        per_device,
        mesh=mesh,
        in_specs=(
            P(("row", "col"), None),
            P("row", "col", None, None, None),
            P("row", "col", None, None),
            P("row", "col"),
        ),
        out_specs=(P(("row", "col"), None), P(("row", "col"), None)),
        check_vma=False,
    )
```

```python
import functools
import math

import jax
import jax.numpy as jnp
from jax import lax
from jax.experimental import pallas as pl
from jax.experimental.pallas import tpu as pltpu
from jax.sharding import PartitionSpec as P

ITERS = 3
EPSILON = 1e-06
STEP_SIZE = 0.5
MOMENTUM = 0.5

SUB = 8
F32 = jnp.float32
BF16 = jnp.bfloat16
HIGHEST = lax.Precision.HIGHEST
VMEM = pl.BlockSpec(memory_space=pltpu.VMEM)
SMEM = pl.BlockSpec(memory_space=pltpu.SMEM)
SPARE_BYTES = 6 * 2**20


def nbytes(shape, dtype):
    return math.prod(shape) * jnp.dtype(dtype).itemsize


def call(body, outputs, scratch=(), smem=1, inputs=0):
    def run(*operands):
        held = sum(nbytes(x.shape, x.dtype) for x in operands)
        held += sum(nbytes(*output) for output in outputs)
        held += sum(nbytes(x.shape, x.dtype) for x in scratch)
        return pl.pallas_call(
            body,
            out_shape=[jax.ShapeDtypeStruct(shape, dtype) for shape, dtype in outputs],
            in_specs=[SMEM] * smem + [VMEM] * (inputs - smem),
            out_specs=[VMEM] * len(outputs),
            scratch_shapes=list(scratch),
            compiler_params=pltpu.CompilerParams(vmem_limit_bytes=held + SPARE_BYTES),
        )(*operands)

    return run


def dot(left, right, contract=((1,), (0,)), precision=HIGHEST):
    return lax.dot_general(
        left, right, (contract, ((), ())), precision=precision, preferred_element_type=F32
    )


def swap(value, axis, distance):
    size = lax.axis_size(axis)
    return lax.ppermute(value, axis, [(i, i ^ distance) for i in range(size)])


def spread(value):
    return [value] + [swap(value, "col", k) for k in range(2, lax.axis_size("col"), 2)]


def plane_sum(keep, send, rider=None):
    half = keep + swap(send, "col", 1)
    if rider is not None:
        half, rider = lax.optimization_barrier((half, rider))
    total = functools.reduce(jnp.add, spread(half))
    pieces = None if rider is None else spread(rider)
    return total, swap(total, "col", 1), pieces


def sub(x, k):
    return jnp.broadcast_to(x[k : k + 1, :], x.shape)


def lane(x, j):
    return jnp.broadcast_to(x[:, j : j + 1], x.shape)


def factor(matrix, want_upper=False):
    edge = matrix.shape[0]
    blocks = edge // SUB
    shape = (SUB, edge)
    rows = [matrix[SUB * b : SUB * b + SUB, :] for b in range(blocks)]
    sublane = lax.broadcasted_iota(jnp.int32, shape, 0)
    column = lax.broadcasted_iota(jnp.int32, shape, 1)
    at = [sublane == k for k in range(SUB)]
    below = [sublane > k for k in range(SUB)]
    upper_out, inverse_out = [], []
    cols = [lane(rows[0], k) for k in range(SUB)]
    for b in range(blocks):
        here, base = rows[b], SUB * b
        block = (column >= base) & (column < base + SUB)
        more = b + 1 < blocks
        if more:
            first = [lane(rows[b + 1], base + k) for k in range(SUB)]
            ahead = [lane(rows[b + 1], base + SUB + k) for k in range(SUB)]
            terms = list(first)
        unit = jnp.where(column == sublane + base, 1.0, 0.0).astype(F32)
        both = jnp.where(block, unit, here)
        forward, upper = both, here
        pivot = pivot_inv = jnp.ones(shape, F32)
        for k in range(SUB):
            spread = sub(cols[k], k)
            inv = 1.0 / spread
            pivot = jnp.where(at[k], spread, pivot)
            pivot_inv = jnp.where(at[k], inv, pivot_inv)
            others = jnp.where(at[k], 0.0, cols[k])
            heads = {j: sub(cols[j], k) for j in range(k + 1, SUB)}
            for j in range(k + 1, SUB):
                cols[j] = cols[j] - (others * heads[j]) * inv
            if more:
                scale = terms[k] * inv
                for j in range(k + 1, SUB):
                    terms[j] = terms[j] - scale * heads[j]
                for j in range(SUB):
                    ahead[j] = ahead[j] - scale * sub(terms[k], j)
            factors = others * inv
            row = sub(forward, k)
            both = both - factors * row
            if k < SUB - 1:
                low = jnp.where(below[k], factors, 0.0)
                if want_upper:
                    upper = upper - low * sub(upper, k)
                forward = forward - low * row
        root = 1.0 / jnp.sqrt(pivot)
        inverse_out.append(jnp.where(column <= sublane + base, forward * root, 0.0))
        if want_upper:
            upper_out.append(jnp.where(column >= sublane + base, upper * root, 0.0))
        if not more:
            break
        solved = both * pivot_inv
        spreads = [sub(solved, k) for k in range(SUB)]
        for p in range(b + 1, blocks):
            weights = first if p == b + 1 else [lane(rows[p], base + k) for k in range(SUB)]
            products = [weights[k] * spreads[k] for k in range(SUB)]
            while len(products) > 1:
                products = [sum(products[i : i + 2]) for i in range(0, len(products), 2)]
            rows[p] = jnp.where(block, 0.0, rows[p]) - products[0]
        cols = ahead
    inverse = jnp.concatenate(inverse_out, axis=0)
    return (jnp.concatenate(upper_out, axis=0) if want_upper else None), inverse


def energy_kernel(sizes, places, counts, tiles, start, message, row_sums, col_sums):
    edge, slots, n_row, n_col, row_pad, unroll = sizes
    count = counts[0, 0]
    row_sums[...] = jnp.zeros_like(row_sums)
    col_sums[...] = jnp.zeros_like(col_sums)
    ones = jnp.ones((SUB, edge), BF16)

    def visit(q, carry):
        for j in range(unroll):
            s = q * unroll + j
            wide = tiles[0, 0, s].astype(F32)
            square = jnp.where(s < count, wide * wide, 0.0)
            high = square.astype(BF16)
            low = (square - high.astype(F32)).astype(BF16)
            by_row = ((1,), (1,))
            by_col = ((1,), (0,))
            fast = lax.Precision.DEFAULT
            u = jnp.minimum(places[0, 0, 0, s], n_row - 1)
            v = jnp.minimum(places[0, 0, 1, s], n_col - 1)
            row_sums[u] += dot(ones, high, by_row, fast) + dot(ones, low, by_row, fast)
            col_sums[v] += dot(ones, high, by_col, fast) + dot(ones, low, by_col, fast)
        return carry

    lax.fori_loop(0, (count + unroll - 1) // unroll, visit, 0)
    message[0:edge, :] = start[...]
    for v in range(n_col):
        message[edge + v : edge + v + 1, :] = col_sums[v, 0:1, :]
    base = edge + n_col
    for u in range(n_row):
        message[base + u : base + u + 1, :] = row_sums[u, 0:1, :]
    for u in range(n_row, row_pad):
        message[base + u : base + u + 1, :] = row_sums[0, 0:1, :]
    column = lax.broadcasted_iota(jnp.int32, (SUB, edge), 1)
    codes = jnp.where(column == slots, count, 0)
    for s in range(slots):
        code = places[0, 0, 0, s] * n_col + places[0, 0, 1, s]
        codes = jnp.where(column == s, code, codes)
    message[base + row_pad :, :] = codes.astype(F32)


def start_kernel(sizes, here, *refs):
    edge, n_row, n_col, row_pad = sizes
    pieces, (basis, keep, send, row_scale, half) = refs[:n_row], refs[n_row:]
    rank, core = here[0], here[1] % 2
    gram = jnp.zeros((edge, edge), F32)
    row_energy = jnp.zeros((row_pad, edge), F32)
    part = n_row * n_col // 2
    for k in range(n_row):
        group = rank ^ k
        rows = pieces[k][0:edge, :]
        basis[pl.ds(pl.multiple_of(group * edge, edge), edge), :] = rows
        gram += dot(rows, rows, ((0,), (0,)))
        row_energy += pieces[k][edge + n_col : edge + n_col + row_pad, :]
        half[pl.ds(pl.multiple_of(edge + group * n_col, n_col), n_col), :] = pieces[k][
            edge : edge + n_col, :
        ]
    half[0:edge, :] = gram
    low = jnp.concatenate([half[0 : edge // 2, :], half[edge : edge + part, :]], axis=0)
    high = jnp.concatenate([half[edge // 2 : edge, :], half[edge + part :, :]], axis=0)
    keep[...] = jnp.where(core == 0, low, high)
    send[...] = jnp.where(core == 0, high, low)
    scale = inverse_fourth_root(row_energy)
    for u in range(n_row):
        row_scale[u * edge : (u + 1) * edge, :] = down_rows(scale[u : u + 1, :], edge)


def inverse_fourth_root(energy):
    return 1.0 / jnp.sqrt(jnp.sqrt(energy + EPSILON))


def down_rows(row, edge):
    return jnp.transpose(jnp.broadcast_to(row, (edge, edge)))


def halves(here, mine, other):
    core = here[1] % 2
    own, sibling = mine[...], other[...]
    return jnp.where(core == 0, own, sibling), jnp.where(core == 0, sibling, own)


def first_factor_kernel(sizes, here, mine, other, inverse, energy):
    edge, items = sizes
    low, high = halves(here, mine, other)
    half = edge // 2
    energy[...] = jnp.concatenate([low[half:], high[half:]], axis=0)
    gram = jnp.concatenate([low[:half], high[:half]], axis=0) / items
    inverse[...] = factor(gram)[1]


def first_update_kernel(sizes, distance, here, inverse, energy, piece, new, scaled, col_scale):
    edge, n_row, n_col = sizes
    for u in range(n_row):
        row = energy[pl.ds(u * n_col + (here[1] ^ distance), 1), :]
        col_scale[u * edge : (u + 1) * edge, :] = down_rows(inverse_fourth_root(row), edge)
    value = dot(piece[...], inverse[...], ((1,), (1,)))
    new[...] = value
    scaled[...] = (col_scale[...] * value).astype(BF16)


def apply_kernel(sizes, first, meta, here, row_scale, current, previous, *refs):
    edge, slots, n_row, n_col, unroll = sizes
    tiles, scaled = refs[: 2 * n_row], refs[2 * n_row : 2 * n_row + n_col]
    value, keep, send, panels, total = refs[2 * n_row + n_col :]
    rank, place = here[0], here[1]
    for k in range(n_col):
        panels[place ^ k] = scaled[k][...].reshape(n_row, edge, edge)
    total[...] = jnp.zeros_like(total)
    width = slots + 1
    for k in range(n_row):
        group = rank ^ k
        for part in range(2):
            begin = part * tiles[0].shape[2]
            live = jnp.clip(meta[k * width + slots] - begin, 0, tiles[part].shape[2])

            def visit(q, carry, k=k, group=group, part=part, begin=begin, live=live):
                for j in range(unroll):
                    s = q * unroll + j
                    code = meta[k * width + begin + s]
                    u = jnp.minimum(code // n_col, n_row - 1)
                    v = code % n_col
                    product = dot(
                        tiles[2 * k + part][0, 0, s],
                        panels[v, group],
                        precision=lax.Precision.DEFAULT,
                    )
                    total[u] += jnp.where(s < live, product, 0.0)
                return carry

            lax.fori_loop(0, (live + unroll - 1) // unroll, visit, 0)
    applied = row_scale[...] * total[...].reshape(n_row * edge, edge)
    moved = applied if first else applied + MOMENTUM * previous[...]
    value[...] = moved
    cross = dot(current[...], moved, ((0,), (0,)))
    square = dot(moved, moved, ((0,), (0,)))
    core = place % 2
    keep[...] = jnp.where(core == 0, cross, square)
    send[...] = jnp.where(core == 0, square, cross)


def moved_gram(cross, square):
    edge = cross.shape[0]
    shape = (edge, edge)
    row = lax.broadcasted_iota(jnp.int32, shape, 0)
    column = lax.broadcasted_iota(jnp.int32, shape, 1)
    identity = jnp.where(row == column, 1.0, 0.0).astype(F32)
    change = square - dot(cross, cross, ((0,), (0,)))
    return identity + STEP_SIZE * STEP_SIZE * change


def factor_kernel(sizes, here, mine, other, *refs):
    count, items = sizes
    currents, inverse_out, bases, coupling = (
        refs[:count],
        refs[count],
        refs[count + 1 : 2 * count + 1],
        refs[2 * count + 1 :],
    )
    cross, square = halves(here, mine, other)
    cross, square = cross / items, square / items
    upper, inverse = factor(moved_gram(cross, square), bool(coupling))
    for current, base in zip(currents, bases):
        base[...] = current[...] - STEP_SIZE * dot(current[...], cross)
    inverse_out[...] = inverse
    if coupling:
        coupling[0][...] = (upper - inverse) / STEP_SIZE


def update_kernel(inverse, base, value, col_scale, current, scaled, *others):
    moved = base[...] + STEP_SIZE * value[...]
    result = dot(moved, inverse[...], ((1,), (1,)))
    scaled[...] = (col_scale[...] * result).astype(BF16)
    if others:
        others[0][...] = result
    if len(others) > 1:
        others[1][...] = (moved - current[...]) / STEP_SIZE


def last_kernel(
    sizes, here, mine, other, current, value, previous, coupling, basis, residual
):
    edge, items = sizes
    cross, square = halves(here, mine, other)
    cross, square = cross / items, square / items
    rows = pl.ds(pl.multiple_of(here[0] * edge, edge), edge)
    old, moved = current[rows, :], value[rows, :]
    rayleigh = cross - MOMENTUM * coupling[...]
    residual[...] = moved - MOMENTUM * previous[rows, :] - dot(old, rayleigh)
    step = moved - dot(old, cross)
    _, inverse = factor(moved_gram(cross, square))
    basis[...] = dot(old + STEP_SIZE * step, inverse, ((1,), (1,)))


def per_device(start_basis, tile_values, tile_coords, tile_count):
    edge, columns = start_basis.shape
    slots = tile_values.shape[2]
    n_row, n_col = lax.axis_size("row"), lax.axis_size("col")
    items = float(edge * n_row * n_col)
    rows = n_row * edge
    row_pad = -(-n_row // SUB) * SUB
    here = jnp.stack([lax.axis_index("row"), lax.axis_index("col")]).astype(jnp.int32)
    block = ((rows, columns), F32)
    square = ((columns, columns), F32)

    first = slots * 4 // 16
    halves_here = (tile_values[:, :, :first], tile_values[:, :, first:])
    early, late = ([half] + [None] * (n_row - 1) for half in halves_here)
    direct = [k for k in range(1, n_row) if k & (k - 1) == 0]
    relayed = [k for k in range(1, n_row) if k & (k - 1) != 0]
    for k in direct:
        early[k] = swap(early[0], "row", k)

    length = edge + n_col + row_pad + SUB
    (message,) = call(
        functools.partial(energy_kernel, (edge, slots, n_row, n_col, row_pad, 4)),
        [((length, columns), F32)],
        [pltpu.VMEM((n_row, SUB, columns), F32), pltpu.VMEM((n_col, SUB, columns), F32)],
        smem=2,
        inputs=4,
    )(tile_coords, tile_count, tile_values, start_basis)
    messages = [message] + [swap(message, "row", k) for k in range(1, n_row)]
    messages, early, late[0] = lax.optimization_barrier((messages, early, late[0]))
    for k in relayed:
        early[k] = swap(early[k & (k - 1)], "row", k & -k)
    for k in direct:
        late[k] = swap(late[0], "row", k)
    meta = jnp.concatenate([m[length - SUB, : slots + 1] for m in messages]).astype(jnp.int32)

    part = (edge + n_row * n_col) // 2
    basis, keep, send, row_scale = call(
        functools.partial(start_kernel, (edge, n_row, n_col, row_pad)),
        [block, ((part, columns), F32), ((part, columns), F32), block],
        [pltpu.VMEM((2 * part, columns), F32)],
        inputs=1 + n_row,
    )(here, *messages)
    mine, other, pieces = plane_sum(keep, send, basis)
    mine, late = lax.optimization_barrier((mine, late))
    for k in relayed:
        late[k] = swap(late[k & (k - 1)], "row", k & -k)
    tiles = [half for pair in zip(early, late) for half in pair]

    count = n_col // 2
    piece_rows = ((rows, columns), BF16)
    inverse, energy = call(
        functools.partial(first_factor_kernel, (edge, items)),
        [square, ((n_row * n_col, columns), F32)],
        inputs=3,
    )(here, mine, other)
    firsts = [
        call(
            functools.partial(first_update_kernel, (edge, n_row, n_col), 2 * i),
            [block, piece_rows, block],
            inputs=4,
        )(here, inverse, energy, piece)
        for i, piece in enumerate(pieces)
    ]
    currents, scaled, col_scales = (list(part) for part in zip(*firsts))
    previous = basis
    for iteration in range(ITERS):
        first, final = iteration == 0, iteration == ITERS - 1
        panels = [part for piece in scaled for part in (piece, swap(piece, "col", 1))]
        value, keep, send = call(
            functools.partial(apply_kernel, (edge, slots, n_row, n_col, 4), first),
            [block, square, square],
            [
                pltpu.VMEM((n_col, n_row, edge, columns), BF16),
                pltpu.VMEM((n_row, edge, columns), F32),
            ],
            smem=2,
            inputs=5 + 2 * n_row + n_col,
        )(meta, here, row_scale, currents[0], previous, *tiles, *panels)
        mine, other, values = plane_sum(keep, send, None if final else value)
        if final:
            break
        inverse, *rest = call(
            functools.partial(factor_kernel, (count, items)),
            [square] + [block] * count + [square] * (iteration == ITERS - 2),
            inputs=3 + count,
        )(here, mine, other, *currents)
        bases, coupling = rest[:count], rest[count:]
        wanted = [2] + [0 if iteration == ITERS - 2 else 1] * (count - 1)
        updates = [
            call(update_kernel, [piece_rows] + [block] * wanted[i], smem=0, inputs=5)(
                inverse, bases[i], values[i], col_scales[i], currents[i]
            )
            for i in range(count)
        ]
        scaled = [u[0] for u in updates]
        previous = updates[0][2]
        currents = [u[1] for u in updates if len(u) > 1]
    basis, residual = call(
        functools.partial(last_kernel, (edge, items)),
        [((edge, columns), F32), ((edge, columns), F32)],
        inputs=7,
    )(here, mine, other, currents[0], value, previous, *coupling)
    return (basis, residual)


def solution(mesh):
    return jax.shard_map(
        per_device,
        mesh=mesh,
        in_specs=(
            P(("row", "col"), None),
            P("row", "col", None, None, None),
            P("row", "col", None, None),
            P("row", "col"),
        ),
        out_specs=(P(("row", "col"), None), P(("row", "col"), None)),
        check_vma=False,
    )
```

```python
import functools
import math

import jax
import jax.numpy as jnp
from jax import lax
from jax.experimental import pallas as pl
from jax.experimental.pallas import tpu as pltpu
from jax.sharding import PartitionSpec as P

ITERS = 3
EPSILON = 1e-06
STEP_SIZE = 0.5
MOMENTUM = 0.5

SUB = 8
F32 = jnp.float32
BF16 = jnp.bfloat16
HIGHEST = lax.Precision.HIGHEST
VMEM = pl.BlockSpec(memory_space=pltpu.VMEM)
SMEM = pl.BlockSpec(memory_space=pltpu.SMEM)
SPARE_BYTES = 6 * 2**20


def nbytes(shape, dtype):
    return math.prod(shape) * jnp.dtype(dtype).itemsize


def call(body, outputs, scratch=(), smem=1, inputs=0):
    def run(*operands):
        held = sum(nbytes(x.shape, x.dtype) for x in operands)
        held += sum(nbytes(*output) for output in outputs)
        held += sum(nbytes(x.shape, x.dtype) for x in scratch)
        return pl.pallas_call(
            body,
            out_shape=[jax.ShapeDtypeStruct(shape, dtype) for shape, dtype in outputs],
            in_specs=[SMEM] * smem + [VMEM] * (inputs - smem),
            out_specs=[VMEM] * len(outputs),
            scratch_shapes=list(scratch),
            compiler_params=pltpu.CompilerParams(vmem_limit_bytes=held + SPARE_BYTES),
        )(*operands)

    return run


def dot(left, right, contract=((1,), (0,)), precision=HIGHEST):
    return lax.dot_general(
        left, right, (contract, ((), ())), precision=precision, preferred_element_type=F32
    )


def split(value):
    high = value.astype(BF16)
    return high, (value - high.astype(F32)).astype(BF16)


def products(left, right):
    left_high, left_low = split(left)
    high, low = split(right)
    rows = jnp.concatenate([left_high, high, left_low, low], axis=1)
    both = jnp.concatenate([high, low], axis=1)
    result = dot(rows, both, ((0,), (0,)), lax.Precision.DEFAULT)
    half, edge = rows.shape[1] // 2, high.shape[1]
    return result[:half, :edge] + (result[half:, :edge] + result[:half, edge:])


def swap(value, axis, distance):
    size = lax.axis_size(axis)
    return lax.ppermute(value, axis, [(i, i ^ distance) for i in range(size)])


def spread(value, distances):
    return [swap(value, "col", k) if k else value for k in distances]


def parity_distances():
    return list(range(0, lax.axis_size("col"), 2))


def near_distances():
    return [k for k in parity_distances() if k & (k - 1) == 0]


def plane_sum(keep, send, rider=None, distances=()):
    half = keep + swap(send, "col", 1)
    if rider is not None:
        half, rider = lax.optimization_barrier((half, rider))
    total = functools.reduce(jnp.add, spread(half, parity_distances()))
    pieces = None if rider is None else spread(rider, distances)
    return total, swap(total, "col", 1), pieces


def plane_panels(scaled):
    for k in parity_distances():
        if k not in scaled:
            scaled = {**scaled, k: swap(scaled[k & (k - 1)], "col", k & -k)}
    return [part for k in parity_distances() for part in (scaled[k], swap(scaled[k], "col", 1))]


def sub(x, k):
    return jnp.broadcast_to(x[k : k + 1, :], x.shape)


def lane(x, j):
    return jnp.broadcast_to(x[:, j : j + 1], x.shape)


def factor(matrix, want_upper=False):
    edge = matrix.shape[0]
    blocks = edge // SUB
    shape = (SUB, edge)
    rows = [matrix[SUB * b : SUB * b + SUB, :] for b in range(blocks)]
    sublane = lax.broadcasted_iota(jnp.int32, shape, 0)
    column = lax.broadcasted_iota(jnp.int32, shape, 1)
    at = [sublane == k for k in range(SUB)]
    below = [sublane > k for k in range(SUB)]
    upper_out, inverse_out = [], []
    cols = [lane(rows[0], k) for k in range(SUB)]
    for b in range(blocks):
        here, base = rows[b], SUB * b
        block = (column >= base) & (column < base + SUB)
        more = b + 1 < blocks
        if more:
            first = [lane(rows[b + 1], base + k) for k in range(SUB)]
            ahead = [lane(rows[b + 1], base + SUB + k) for k in range(SUB)]
            terms = list(first)
        unit = jnp.where(column == sublane + base, 1.0, 0.0).astype(F32)
        both = jnp.where(block, unit, here)
        forward, upper = both, here
        pivot = pivot_inv = jnp.ones(shape, F32)
        for k in range(SUB):
            spread = sub(cols[k], k)
            inv = 1.0 / spread
            pivot = jnp.where(at[k], spread, pivot)
            pivot_inv = jnp.where(at[k], inv, pivot_inv)
            others = jnp.where(at[k], 0.0, cols[k])
            heads = {j: sub(cols[j], k) for j in range(k + 1, SUB)}
            for j in range(k + 1, SUB):
                cols[j] = cols[j] - (others * heads[j]) * inv
            if more:
                scale = terms[k] * inv
                for j in range(k + 1, SUB):
                    terms[j] = terms[j] - scale * heads[j]
                for j in range(SUB):
                    ahead[j] = ahead[j] - scale * sub(terms[k], j)
            factors = others * inv
            row = sub(forward, k)
            both = both - factors * row
            if k < SUB - 1:
                low = jnp.where(below[k], factors, 0.0)
                if want_upper:
                    upper = upper - low * sub(upper, k)
                forward = forward - low * row
        root = 1.0 / jnp.sqrt(pivot)
        inverse_out.append(jnp.where(column <= sublane + base, forward * root, 0.0))
        if want_upper:
            upper_out.append(jnp.where(column >= sublane + base, upper * root, 0.0))
        if not more:
            break
        solved = both * pivot_inv
        spreads = [sub(solved, k) for k in range(SUB)]
        for p in range(b + 1, blocks):
            weights = first if p == b + 1 else [lane(rows[p], base + k) for k in range(SUB)]
            products = [weights[k] * spreads[k] for k in range(SUB)]
            while len(products) > 1:
                products = [sum(products[i : i + 2]) for i in range(0, len(products), 2)]
            rows[p] = jnp.where(block, 0.0, rows[p]) - products[0]
        cols = ahead
    inverse = jnp.concatenate(inverse_out, axis=0)
    return (jnp.concatenate(upper_out, axis=0) if want_upper else None), inverse


def energy_kernel(sizes, places, counts, tiles, start, message, row_sums, col_sums):
    edge, slots, n_row, n_col, row_pad, unroll = sizes
    count = counts[0, 0]
    row_sums[...] = jnp.zeros_like(row_sums)
    col_sums[...] = jnp.zeros_like(col_sums)
    ones = jnp.ones((SUB, edge), BF16)

    def visit(q, carry):
        for j in range(unroll):
            s = q * unroll + j
            wide = tiles[0, 0, s].astype(F32)
            square = jnp.where(s < count, wide * wide, 0.0)
            high = square.astype(BF16)
            low = (square - high.astype(F32)).astype(BF16)
            by_row = ((1,), (1,))
            by_col = ((1,), (0,))
            fast = lax.Precision.DEFAULT
            u = jnp.minimum(places[0, 0, 0, s], n_row - 1)
            v = jnp.minimum(places[0, 0, 1, s], n_col - 1)
            row_sums[u] += dot(ones, high, by_row, fast) + dot(ones, low, by_row, fast)
            col_sums[v] += dot(ones, high, by_col, fast) + dot(ones, low, by_col, fast)
        return carry

    lax.fori_loop(0, (count + unroll - 1) // unroll, visit, 0)
    message[0:edge, :] = start[...]
    for v in range(n_col):
        message[edge + v : edge + v + 1, :] = col_sums[v, 0:1, :]
    base = edge + n_col
    for u in range(n_row):
        message[base + u : base + u + 1, :] = row_sums[u, 0:1, :]
    for u in range(n_row, row_pad):
        message[base + u : base + u + 1, :] = row_sums[0, 0:1, :]
    column = lax.broadcasted_iota(jnp.int32, (SUB, edge), 1)
    codes = jnp.where(column == slots, count, 0)
    for s in range(slots):
        code = places[0, 0, 0, s] * n_col + places[0, 0, 1, s]
        codes = jnp.where(column == s, code, codes)
    message[base + row_pad :, :] = codes.astype(F32)


def start_kernel(sizes, here, *refs):
    edge, n_row, n_col, row_pad = sizes
    pieces, (basis, keep, send, row_scale, half) = refs[:n_row], refs[n_row:]
    rank, core = here[0], here[1] % 2
    gram = jnp.zeros((edge, edge), F32)
    row_energy = jnp.zeros((row_pad, edge), F32)
    part = n_row * n_col // 2
    for k in range(n_row):
        group = rank ^ k
        rows = pieces[k][0:edge, :]
        basis[pl.ds(pl.multiple_of(group * edge, edge), edge), :] = rows
        gram += dot(rows, rows, ((0,), (0,)))
        row_energy += pieces[k][edge + n_col : edge + n_col + row_pad, :]
        half[pl.ds(pl.multiple_of(edge + group * n_col, n_col), n_col), :] = pieces[k][
            edge : edge + n_col, :
        ]
    half[0:edge, :] = gram
    low = jnp.concatenate([half[0 : edge // 2, :], half[edge : edge + part, :]], axis=0)
    high = jnp.concatenate([half[edge // 2 : edge, :], half[edge + part :, :]], axis=0)
    keep[...] = jnp.where(core == 0, low, high)
    send[...] = jnp.where(core == 0, high, low)
    scale = inverse_fourth_root(row_energy)
    for u in range(n_row):
        row_scale[u * edge : (u + 1) * edge, :] = down_rows(scale[u : u + 1, :], edge)


def inverse_fourth_root(energy):
    return 1.0 / jnp.sqrt(jnp.sqrt(energy + EPSILON))


def down_rows(row, edge):
    return jnp.transpose(jnp.broadcast_to(row, (edge, edge)))


def halves(here, mine, other):
    core = here[1] % 2
    own, sibling = mine[...], other[...]
    return jnp.where(core == 0, own, sibling), jnp.where(core == 0, sibling, own)


def first_factor_kernel(sizes, here, mine, other, inverse, energy):
    edge, items = sizes
    low, high = halves(here, mine, other)
    half = edge // 2
    energy[...] = jnp.concatenate([low[half:], high[half:]], axis=0)
    gram = jnp.concatenate([low[:half], high[:half]], axis=0) / items
    inverse[...] = factor(gram)[1]


def first_update_kernel(sizes, distance, here, inverse, energy, piece, new, scaled, col_scale):
    edge, n_row, n_col = sizes
    for u in range(n_row):
        row = energy[pl.ds(u * n_col + (here[1] ^ distance), 1), :]
        col_scale[u * edge : (u + 1) * edge, :] = down_rows(inverse_fourth_root(row), edge)
    value = dot(piece[...], inverse[...], ((1,), (1,)))
    new[...] = value
    scaled[...] = (col_scale[...] * value).astype(BF16)


def apply_kernel(sizes, first, meta, here, row_scale, current, previous, *refs):
    edge, slots, n_row, n_col, unroll = sizes
    tiles, scaled = refs[: 2 * n_row], refs[2 * n_row : 2 * n_row + n_col]
    value, keep, send, panels, total = refs[2 * n_row + n_col :]
    rank, place = here[0], here[1]
    for k in range(n_col):
        panels[place ^ k] = scaled[k][...].reshape(n_row, edge, edge)
    total[...] = jnp.zeros_like(total)
    width = slots + 1
    for k in range(n_row):
        group = rank ^ k
        for part in range(2):
            begin = part * tiles[0].shape[2]
            live = jnp.clip(meta[k * width + slots] - begin, 0, tiles[part].shape[2])

            def visit(q, carry, k=k, group=group, part=part, begin=begin, live=live):
                for j in range(unroll):
                    s = q * unroll + j
                    code = meta[k * width + begin + s]
                    u = jnp.minimum(code // n_col, n_row - 1)
                    v = code % n_col
                    product = dot(
                        tiles[2 * k + part][0, 0, s],
                        panels[v, group],
                        precision=lax.Precision.DEFAULT,
                    )
                    total[u] += jnp.where(s < live, product, 0.0)
                return carry

            lax.fori_loop(0, (live + unroll - 1) // unroll, visit, 0)
    applied = row_scale[...] * total[...].reshape(n_row * edge, edge)
    moved = applied if first else applied + MOMENTUM * previous[...]
    value[...] = moved
    parts = products(current[...], moved)
    cross, square = parts[:edge], parts[edge:]
    core = place % 2
    keep[...] = jnp.where(core == 0, cross, square)
    send[...] = jnp.where(core == 0, square, cross)


def moved_gram(cross, square):
    edge = cross.shape[0]
    shape = (edge, edge)
    row = lax.broadcasted_iota(jnp.int32, shape, 0)
    column = lax.broadcasted_iota(jnp.int32, shape, 1)
    identity = jnp.where(row == column, 1.0, 0.0).astype(F32)
    change = square - dot(cross, cross, ((0,), (0,)))
    return identity + STEP_SIZE * STEP_SIZE * change


def factor_kernel(sizes, here, mine, other, *refs):
    count, items = sizes
    currents, inverse_out, bases, coupling = (
        refs[:count],
        refs[count],
        refs[count + 1 : 2 * count + 1],
        refs[2 * count + 1 :],
    )
    cross, square = halves(here, mine, other)
    cross, square = cross / items, square / items
    upper, inverse = factor(moved_gram(cross, square), bool(coupling))
    for current, base in zip(currents, bases):
        base[...] = current[...] - STEP_SIZE * dot(current[...], cross)
    inverse_out[...] = inverse
    if coupling:
        coupling[0][...] = (upper - inverse) / STEP_SIZE


def update_kernel(inverse, base, value, col_scale, current, scaled, *others):
    moved = base[...] + STEP_SIZE * value[...]
    result = dot(moved, inverse[...], ((1,), (1,)))
    scaled[...] = (col_scale[...] * result).astype(BF16)
    if others:
        others[0][...] = result
    if len(others) > 1:
        others[1][...] = (moved - current[...]) / STEP_SIZE


def last_kernel(
    sizes, here, mine, other, current, value, previous, coupling, basis, residual
):
    edge, items = sizes
    cross, square = halves(here, mine, other)
    cross, square = cross / items, square / items
    rows = pl.ds(pl.multiple_of(here[0] * edge, edge), edge)
    old, moved = current[rows, :], value[rows, :]
    rayleigh = cross - MOMENTUM * coupling[...]
    _, inverse = factor(moved_gram(cross, square))
    residual[...] = moved - MOMENTUM * previous[rows, :] - dot(old, rayleigh)
    step = moved - dot(old, cross)
    basis[...] = dot(old + STEP_SIZE * step, inverse, ((1,), (1,)))


def per_device(start_basis, tile_values, tile_coords, tile_count):
    edge, columns = start_basis.shape
    slots = tile_values.shape[2]
    n_row, n_col = lax.axis_size("row"), lax.axis_size("col")
    items = float(edge * n_row * n_col)
    rows = n_row * edge
    row_pad = -(-n_row // SUB) * SUB
    here = jnp.stack([lax.axis_index("row"), lax.axis_index("col")]).astype(jnp.int32)
    block = ((rows, columns), F32)
    square = ((columns, columns), F32)

    first = slots * 4 // 16
    halves_here = (tile_values[:, :, :first], tile_values[:, :, first:])
    early, late = ([half] + [None] * (n_row - 1) for half in halves_here)
    direct = [k for k in range(1, n_row) if k & (k - 1) == 0]
    relayed = [k for k in range(1, n_row) if k & (k - 1) != 0]
    for k in direct:
        early[k] = swap(early[0], "row", k)

    length = edge + n_col + row_pad + SUB
    (message,) = call(
        functools.partial(energy_kernel, (edge, slots, n_row, n_col, row_pad, 4)),
        [((length, columns), F32)],
        [pltpu.VMEM((n_row, SUB, columns), F32), pltpu.VMEM((n_col, SUB, columns), F32)],
        smem=2,
        inputs=4,
    )(tile_coords, tile_count, tile_values, start_basis)
    messages = [message] + [swap(message, "row", k) for k in range(1, n_row)]
    messages, early, late[0] = lax.optimization_barrier((messages, early, late[0]))
    for k in relayed:
        early[k] = swap(early[k & (k - 1)], "row", k & -k)
    for k in direct:
        late[k] = swap(late[0], "row", k)
    meta = jnp.concatenate([m[length - SUB, : slots + 1] for m in messages]).astype(jnp.int32)

    part = (edge + n_row * n_col) // 2
    basis, keep, send, row_scale = call(
        functools.partial(start_kernel, (edge, n_row, n_col, row_pad)),
        [block, ((part, columns), F32), ((part, columns), F32), block],
        [pltpu.VMEM((2 * part, columns), F32)],
        inputs=1 + n_row,
    )(here, *messages)
    everywhere, near = parity_distances(), near_distances()
    mine, other, pieces = plane_sum(keep, send, basis, everywhere)
    mine, late = lax.optimization_barrier((mine, late))
    for k in relayed:
        late[k] = swap(late[k & (k - 1)], "row", k & -k)
    tiles = [half for pair in zip(early, late) for half in pair]

    count = len(near)
    piece_rows = ((rows, columns), BF16)
    inverse, energy = call(
        functools.partial(first_factor_kernel, (edge, items)),
        [square, ((n_row * n_col, columns), F32)],
        inputs=3,
    )(here, mine, other)
    firsts = [
        call(
            functools.partial(first_update_kernel, (edge, n_row, n_col), distance),
            [block, piece_rows, block],
            inputs=4,
        )(here, inverse, energy, piece)
        for distance, piece in zip(everywhere, pieces)
    ]
    scaled = {k: f[1] for k, f in zip(everywhere, firsts)}
    currents, _, col_scales = zip(*[f for k, f in zip(everywhere, firsts) if k in near])
    previous = basis
    for iteration in range(ITERS):
        first, final = iteration == 0, iteration == ITERS - 1
        panels = plane_panels(scaled)
        value, keep, send = call(
            functools.partial(apply_kernel, (edge, slots, n_row, n_col, 4), first),
            [block, square, square],
            [
                pltpu.VMEM((n_col, n_row, edge, columns), BF16),
                pltpu.VMEM((n_row, edge, columns), F32),
            ],
            smem=2,
            inputs=5 + 2 * n_row + n_col,
        )(meta, here, row_scale, currents[0], previous, *tiles, *panels)
        mine, other, values = plane_sum(keep, send, None if final else value, near)
        if final:
            break
        inverse, *rest = call(
            functools.partial(factor_kernel, (count, items)),
            [square] + [block] * count + [square] * (iteration == ITERS - 2),
            inputs=3 + count,
        )(here, mine, other, *currents)
        bases, coupling = rest[:count], rest[count:]
        wanted = [2] + [0 if iteration == ITERS - 2 else 1] * (count - 1)
        updates = [
            call(update_kernel, [piece_rows] + [block] * wanted[i], smem=0, inputs=5)(
                inverse, bases[i], values[i], col_scales[i], currents[i]
            )
            for i in range(count)
        ]
        scaled = {k: u[0] for k, u in zip(near, updates)}
        previous = updates[0][2]
        currents = [u[1] for u in updates if len(u) > 1]
    basis, residual = call(
        functools.partial(last_kernel, (edge, items)),
        [((edge, columns), F32), ((edge, columns), F32)],
        inputs=7,
    )(here, mine, other, currents[0], value, previous, *coupling)
    return (basis, residual)


def solution(mesh):
    return jax.shard_map(
        per_device,
        mesh=mesh,
        in_specs=(
            P(("row", "col"), None),
            P("row", "col", None, None, None),
            P("row", "col", None, None),
            P("row", "col"),
        ),
        out_specs=(P(("row", "col"), None), P(("row", "col"), None)),
        check_vma=False,
    )
```

```python
import functools
import math

import jax
import jax.numpy as jnp
from jax import lax
from jax.experimental import pallas as pl
from jax.experimental.pallas import tpu as pltpu
from jax.sharding import PartitionSpec as P

ITERS = 3
EPSILON = 1e-06
STEP_SIZE = 0.5
MOMENTUM = 0.5

SUB = 8
F32 = jnp.float32
BF16 = jnp.bfloat16
HIGHEST = lax.Precision.HIGHEST
VMEM = pl.BlockSpec(memory_space=pltpu.VMEM)
SMEM = pl.BlockSpec(memory_space=pltpu.SMEM)
SPARE_BYTES = 6 * 2**20


def nbytes(shape, dtype):
    return math.prod(shape) * jnp.dtype(dtype).itemsize


def call(body, outputs, scratch=(), smem=1, inputs=0):
    def run(*operands):
        held = sum(nbytes(x.shape, x.dtype) for x in operands)
        held += sum(nbytes(*output) for output in outputs)
        held += sum(nbytes(x.shape, x.dtype) for x in scratch)
        return pl.pallas_call(
            body,
            out_shape=[jax.ShapeDtypeStruct(shape, dtype) for shape, dtype in outputs],
            in_specs=[SMEM] * smem + [VMEM] * (inputs - smem),
            out_specs=[VMEM] * len(outputs),
            scratch_shapes=list(scratch),
            compiler_params=pltpu.CompilerParams(vmem_limit_bytes=held + SPARE_BYTES),
        )(*operands)

    return run


def dot(left, right, contract=((1,), (0,)), precision=HIGHEST):
    return lax.dot_general(
        left, right, (contract, ((), ())), precision=precision, preferred_element_type=F32
    )


def split(value):
    high = value.astype(BF16)
    return high, (value - high.astype(F32)).astype(BF16)


def products(left, right):
    left_high, left_low = split(left)
    high, low = split(right)
    rows = jnp.concatenate([left_high, high, left_low, low], axis=1)
    both = jnp.concatenate([high, low], axis=1)
    result = dot(rows, both, ((0,), (0,)), lax.Precision.DEFAULT)
    half, edge = rows.shape[1] // 2, high.shape[1]
    return result[:half, :edge] + (result[half:, :edge] + result[:half, edge:])


def swap(value, axis, distance):
    size = lax.axis_size(axis)
    return lax.ppermute(value, axis, [(i, i ^ distance) for i in range(size)])


def spread(value, distances):
    return [swap(value, "col", k) if k else value for k in distances]


def parity_distances():
    return list(range(0, lax.axis_size("col"), 2))


def near_distances():
    return [k for k in parity_distances() if k & (k - 1) == 0]


def plane_sum(keep, send, rider=None, distances=()):
    half = keep + swap(send, "col", 1)
    if rider is not None:
        half, rider = lax.optimization_barrier((half, rider))
    total = functools.reduce(jnp.add, spread(half, parity_distances()))
    pieces = None if rider is None else spread(rider, distances)
    return total, swap(total, "col", 1), pieces


def plane_panels(scaled):
    for k in parity_distances():
        if k not in scaled:
            scaled = {**scaled, k: swap(scaled[k & (k - 1)], "col", k & -k)}
    return [part for k in parity_distances() for part in (scaled[k], swap(scaled[k], "col", 1))]


def sub(x, k):
    return jnp.broadcast_to(x[k : k + 1, :], x.shape)


def lane(x, j):
    return jnp.broadcast_to(x[:, j : j + 1], x.shape)


def factor(matrix, want_upper=False):
    edge = matrix.shape[0]
    blocks = edge // SUB
    shape = (SUB, edge)
    rows = [matrix[SUB * b : SUB * b + SUB, :] for b in range(blocks)]
    sublane = lax.broadcasted_iota(jnp.int32, shape, 0)
    column = lax.broadcasted_iota(jnp.int32, shape, 1)
    at = [sublane == k for k in range(SUB)]
    below = [sublane > k for k in range(SUB)]
    upper_out, inverse_out = [], []
    cols = [lane(rows[0], k) for k in range(SUB)]
    for b in range(blocks):
        here, base = rows[b], SUB * b
        block = (column >= base) & (column < base + SUB)
        more = b + 1 < blocks
        if more:
            first = [lane(rows[b + 1], base + k) for k in range(SUB)]
            ahead = [lane(rows[b + 1], base + SUB + k) for k in range(SUB)]
            terms = list(first)
        unit = jnp.where(column == sublane + base, 1.0, 0.0).astype(F32)
        both = jnp.where(block, unit, here)
        forward, upper = both, here
        pivot = pivot_inv = jnp.ones(shape, F32)
        for k in range(SUB):
            spread = sub(cols[k], k)
            inv = 1.0 / spread
            pivot = jnp.where(at[k], spread, pivot)
            pivot_inv = jnp.where(at[k], inv, pivot_inv)
            others = jnp.where(at[k], 0.0, cols[k])
            heads = {j: sub(cols[j], k) for j in range(k + 1, SUB)}
            for j in range(k + 1, SUB):
                cols[j] = cols[j] - (others * heads[j]) * inv
            if more:
                scale = terms[k] * inv
                for j in range(k + 1, SUB):
                    terms[j] = terms[j] - scale * heads[j]
                for j in range(SUB):
                    ahead[j] = ahead[j] - scale * sub(terms[k], j)
            factors = others * inv
            row = sub(forward, k)
            both = both - factors * row
            if k < SUB - 1:
                low = jnp.where(below[k], factors, 0.0)
                if want_upper:
                    upper = upper - low * sub(upper, k)
                forward = forward - low * row
        root = 1.0 / jnp.sqrt(pivot)
        inverse_out.append(jnp.where(column <= sublane + base, forward * root, 0.0))
        if want_upper:
            upper_out.append(jnp.where(column >= sublane + base, upper * root, 0.0))
        if not more:
            break
        solved = both * pivot_inv
        spreads = [sub(solved, k) for k in range(SUB)]
        for p in range(b + 1, blocks):
            weights = first if p == b + 1 else [lane(rows[p], base + k) for k in range(SUB)]
            products = [weights[k] * spreads[k] for k in range(SUB)]
            while len(products) > 1:
                products = [sum(products[i : i + 2]) for i in range(0, len(products), 2)]
            rows[p] = jnp.where(block, 0.0, rows[p]) - products[0]
        cols = ahead
    inverse = jnp.concatenate(inverse_out, axis=0)
    return (jnp.concatenate(upper_out, axis=0) if want_upper else None), inverse


def energy_kernel(sizes, places, counts, tiles, start, message, row_sums, col_sums):
    edge, slots, n_row, n_col, row_pad, unroll = sizes
    count = counts[0, 0]
    row_sums[...] = jnp.zeros_like(row_sums)
    col_sums[...] = jnp.zeros_like(col_sums)
    ones = jnp.ones((SUB, edge), BF16)

    def visit(q, carry):
        for j in range(unroll):
            s = q * unroll + j
            wide = tiles[0, 0, s].astype(F32)
            square = jnp.where(s < count, wide * wide, 0.0)
            high = square.astype(BF16)
            low = (square - high.astype(F32)).astype(BF16)
            by_row = ((1,), (1,))
            by_col = ((1,), (0,))
            fast = lax.Precision.DEFAULT
            u = jnp.minimum(places[0, 0, 0, s], n_row - 1)
            v = jnp.minimum(places[0, 0, 1, s], n_col - 1)
            row_sums[u] += dot(ones, high, by_row, fast) + dot(ones, low, by_row, fast)
            col_sums[v] += dot(ones, high, by_col, fast) + dot(ones, low, by_col, fast)
        return carry

    lax.fori_loop(0, (count + unroll - 1) // unroll, visit, 0)
    message[0:edge, :] = start[...]
    for v in range(n_col):
        message[edge + v : edge + v + 1, :] = col_sums[v, 0:1, :]
    base = edge + n_col
    for u in range(n_row):
        message[base + u : base + u + 1, :] = row_sums[u, 0:1, :]
    for u in range(n_row, row_pad):
        message[base + u : base + u + 1, :] = row_sums[0, 0:1, :]
    column = lax.broadcasted_iota(jnp.int32, (SUB, edge), 1)
    codes = jnp.where(column == slots, count, 0)
    for s in range(slots):
        code = places[0, 0, 0, s] * n_col + places[0, 0, 1, s]
        codes = jnp.where(column == s, code, codes)
    message[base + row_pad :, :] = codes.astype(F32)


def start_kernel(sizes, here, *refs):
    edge, n_row, n_col, row_pad = sizes
    pieces, (basis, keep, send, row_scale, half) = refs[:n_row], refs[n_row:]
    rank, core = here[0], here[1] % 2
    gram = jnp.zeros((edge, edge), F32)
    row_energy = jnp.zeros((row_pad, edge), F32)
    part = n_row * n_col // 2
    for k in range(n_row):
        group = rank ^ k
        rows = pieces[k][0:edge, :]
        basis[pl.ds(pl.multiple_of(group * edge, edge), edge), :] = rows
        gram += dot(rows, rows, ((0,), (0,)))
        row_energy += pieces[k][edge + n_col : edge + n_col + row_pad, :]
        half[pl.ds(pl.multiple_of(edge + group * n_col, n_col), n_col), :] = pieces[k][
            edge : edge + n_col, :
        ]
    half[0:edge, :] = gram
    low = jnp.concatenate([half[0 : edge // 2, :], half[edge : edge + part, :]], axis=0)
    high = jnp.concatenate([half[edge // 2 : edge, :], half[edge + part :, :]], axis=0)
    keep[...] = jnp.where(core == 0, low, high)
    send[...] = jnp.where(core == 0, high, low)
    down_rows(inverse_fourth_root(row_energy), row_scale)


def inverse_fourth_root(energy):
    return 1.0 / jnp.sqrt(jnp.sqrt(energy + EPSILON))


def down_rows(scales, out):
    edge = scales.shape[1]
    columns = jnp.transpose(scales)
    for u in range(out.shape[0] // edge):
        out[u * edge : (u + 1) * edge, :] = jnp.broadcast_to(columns[:, u : u + 1], (edge, edge))


def halves(here, mine, other):
    core = here[1] % 2
    own, sibling = mine[...], other[...]
    return jnp.where(core == 0, own, sibling), jnp.where(core == 0, sibling, own)


def first_factor_kernel(sizes, here, mine, other, inverse, energy):
    edge, items = sizes
    low, high = halves(here, mine, other)
    half = edge // 2
    energy[...] = jnp.concatenate([low[half:], high[half:]], axis=0)
    gram = jnp.concatenate([low[:half], high[:half]], axis=0) / items
    inverse[...] = factor(gram)[1]


def first_update_kernel(sizes, distance, here, inverse, energy, piece, scaled, col_scale, *new):
    edge, n_row, n_col = sizes
    rows = [energy[pl.ds(u * n_col + (here[1] ^ distance), 1), :] for u in range(n_row)]
    rows += rows[:1] * (-n_row % SUB)
    down_rows(inverse_fourth_root(jnp.concatenate(rows, axis=0)), col_scale)
    value = dot(piece[...], inverse[...], ((1,), (1,)))
    scaled[...] = (col_scale[...] * value).astype(BF16)
    if new:
        new[0][...] = value


def apply_kernel(sizes, first, meta, here, row_scale, current, previous, *refs):
    edge, slots, n_row, n_col, unroll = sizes
    tiles, scaled = refs[: 2 * n_row], refs[2 * n_row : 2 * n_row + n_col]
    value, keep, send, panels, total = refs[2 * n_row + n_col :]
    rank, place = here[0], here[1]
    for k in range(n_col):
        panels[place ^ k] = scaled[k][...].reshape(n_row, edge, edge)
    total[...] = jnp.zeros_like(total)
    width = slots + 1
    for k in range(n_row):
        group = rank ^ k
        for part in range(2):
            begin = part * tiles[0].shape[2]
            live = jnp.clip(meta[k * width + slots] - begin, 0, tiles[part].shape[2])

            def visit(q, carry, k=k, group=group, part=part, begin=begin, live=live):
                for j in range(unroll):
                    s = q * unroll + j
                    code = meta[k * width + begin + s]
                    u = jnp.minimum(code // n_col, n_row - 1)
                    v = code % n_col
                    product = dot(
                        tiles[2 * k + part][0, 0, s],
                        panels[v, group],
                        precision=lax.Precision.DEFAULT,
                    )
                    total[u] += jnp.where(s < live, product, 0.0)
                return carry

            lax.fori_loop(0, (live + unroll - 1) // unroll, visit, 0)
    applied = row_scale[...] * total[...].reshape(n_row * edge, edge)
    moved = applied if first else applied + MOMENTUM * previous[...]
    value[...] = moved
    parts = products(current[...], moved)
    cross, square = parts[:edge], parts[edge:]
    core = place % 2
    keep[...] = jnp.where(core == 0, cross, square)
    send[...] = jnp.where(core == 0, square, cross)


def moved_gram(cross, square):
    edge = cross.shape[0]
    shape = (edge, edge)
    row = lax.broadcasted_iota(jnp.int32, shape, 0)
    column = lax.broadcasted_iota(jnp.int32, shape, 1)
    identity = jnp.where(row == column, 1.0, 0.0).astype(F32)
    change = square - dot(cross, cross, ((0,), (0,)))
    return identity + STEP_SIZE * STEP_SIZE * change


def factor_kernel(sizes, here, mine, other, *refs):
    count, items = sizes
    currents, inverse_out, bases, coupling = (
        refs[:count],
        refs[count],
        refs[count + 1 : 2 * count + 1],
        refs[2 * count + 1 :],
    )
    cross, square = halves(here, mine, other)
    cross, square = cross / items, square / items
    upper, inverse = factor(moved_gram(cross, square), bool(coupling))
    for current, base in zip(currents, bases):
        base[...] = current[...] - STEP_SIZE * dot(current[...], cross)
    inverse_out[...] = inverse
    if coupling:
        coupling[0][...] = (upper - inverse) / STEP_SIZE


def update_kernel(inverse, base, value, col_scale, current, scaled, *others):
    moved = base[...] + STEP_SIZE * value[...]
    result = dot(moved, inverse[...], ((1,), (1,)))
    scaled[...] = (col_scale[...] * result).astype(BF16)
    if others:
        others[0][...] = result
    if len(others) > 1:
        others[1][...] = (moved - current[...]) / STEP_SIZE


def last_kernel(
    sizes, here, mine, other, current, value, previous, coupling, basis, residual
):
    edge, items = sizes
    cross, square = halves(here, mine, other)
    cross, square = cross / items, square / items
    rows = pl.ds(pl.multiple_of(here[0] * edge, edge), edge)
    old, moved = current[rows, :], value[rows, :]
    rayleigh = cross - MOMENTUM * coupling[...]
    _, inverse = factor(moved_gram(cross, square))
    residual[...] = moved - MOMENTUM * previous[rows, :] - dot(old, rayleigh)
    step = moved - dot(old, cross)
    basis[...] = dot(old + STEP_SIZE * step, inverse, ((1,), (1,)))


def per_device(start_basis, tile_values, tile_coords, tile_count):
    edge, columns = start_basis.shape
    slots = tile_values.shape[2]
    n_row, n_col = lax.axis_size("row"), lax.axis_size("col")
    items = float(edge * n_row * n_col)
    rows = n_row * edge
    row_pad = -(-n_row // SUB) * SUB
    here = jnp.stack([lax.axis_index("row"), lax.axis_index("col")]).astype(jnp.int32)
    block = ((rows, columns), F32)
    square = ((columns, columns), F32)

    first = slots * 4 // 16
    halves_here = (tile_values[:, :, :first], tile_values[:, :, first:])
    early, late = ([half] + [None] * (n_row - 1) for half in halves_here)
    direct = [k for k in range(1, n_row) if k & (k - 1) == 0]
    relayed = [k for k in range(1, n_row) if k & (k - 1) != 0]
    for k in direct:
        early[k] = swap(early[0], "row", k)

    length = edge + n_col + row_pad + SUB
    (message,) = call(
        functools.partial(energy_kernel, (edge, slots, n_row, n_col, row_pad, 4)),
        [((length, columns), F32)],
        [pltpu.VMEM((n_row, SUB, columns), F32), pltpu.VMEM((n_col, SUB, columns), F32)],
        smem=2,
        inputs=4,
    )(tile_coords, tile_count, tile_values, start_basis)
    messages = [message] + [swap(message, "row", k) for k in range(1, n_row)]
    messages, early, late[0] = lax.optimization_barrier((messages, early, late[0]))
    for k in relayed:
        early[k] = swap(early[k & (k - 1)], "row", k & -k)
    for k in direct:
        late[k] = swap(late[0], "row", k)
    meta = jnp.concatenate([m[length - SUB, : slots + 1] for m in messages]).astype(jnp.int32)

    part = (edge + n_row * n_col) // 2
    basis, keep, send, row_scale = call(
        functools.partial(start_kernel, (edge, n_row, n_col, row_pad)),
        [block, ((part, columns), F32), ((part, columns), F32), block],
        [pltpu.VMEM((2 * part, columns), F32)],
        inputs=1 + n_row,
    )(here, *messages)
    everywhere, near = parity_distances(), near_distances()
    mine, other, pieces = plane_sum(keep, send, basis, everywhere)
    mine, late = lax.optimization_barrier((mine, late))
    for k in relayed:
        late[k] = swap(late[k & (k - 1)], "row", k & -k)
    tiles = [half for pair in zip(early, late) for half in pair]

    count = len(near)
    piece_rows = ((rows, columns), BF16)
    inverse, energy = call(
        functools.partial(first_factor_kernel, (edge, items)),
        [square, ((n_row * n_col, columns), F32)],
        inputs=3,
    )(here, mine, other)
    firsts = {
        k: call(
            functools.partial(first_update_kernel, (edge, n_row, n_col), k),
            [piece_rows, block, block] if k in near else [piece_rows],
            [] if k in near else [pltpu.VMEM(*block)],
            inputs=4,
        )(here, inverse, energy, piece)
        for k, piece in zip(everywhere, pieces)
    }
    scaled = {k: f[0] for k, f in firsts.items()}
    col_scales, currents = zip(*[firsts[k][1:] for k in near])
    previous = basis
    for iteration in range(ITERS):
        first, final = iteration == 0, iteration == ITERS - 1
        panels = plane_panels(scaled)
        value, keep, send = call(
            functools.partial(apply_kernel, (edge, slots, n_row, n_col, 4), first),
            [block, square, square],
            [
                pltpu.VMEM((n_col, n_row, edge, columns), BF16),
                pltpu.VMEM((n_row, edge, columns), F32),
            ],
            smem=2,
            inputs=5 + 2 * n_row + n_col,
        )(meta, here, row_scale, currents[0], previous, *tiles, *panels)
        mine, other, values = plane_sum(keep, send, None if final else value, near)
        if final:
            break
        inverse, *rest = call(
            functools.partial(factor_kernel, (count, items)),
            [square] + [block] * count + [square] * (iteration == ITERS - 2),
            inputs=3 + count,
        )(here, mine, other, *currents)
        bases, coupling = rest[:count], rest[count:]
        wanted = [2] + [0 if iteration == ITERS - 2 else 1] * (count - 1)
        updates = [
            call(update_kernel, [piece_rows] + [block] * wanted[i], smem=0, inputs=5)(
                inverse, bases[i], values[i], col_scales[i], currents[i]
            )
            for i in range(count)
        ]
        scaled = {k: u[0] for k, u in zip(near, updates)}
        previous = updates[0][2]
        currents = [u[1] for u in updates if len(u) > 1]
    basis, residual = call(
        functools.partial(last_kernel, (edge, items)),
        [((edge, columns), F32), ((edge, columns), F32)],
        inputs=7,
    )(here, mine, other, currents[0], value, previous, *coupling)
    return (basis, residual)


def solution(mesh):
    return jax.shard_map(
        per_device,
        mesh=mesh,
        in_specs=(
            P(("row", "col"), None),
            P("row", "col", None, None, None),
            P("row", "col", None, None),
            P("row", "col"),
        ),
        out_specs=(P(("row", "col"), None), P(("row", "col"), None)),
        check_vma=False,
    )
```
